32 devices in a mesh: dp: 2 (over x), expert: 16 (over z, y, core).
Axes of the slice: x: 2, y: 2, z: 4, core: 2. Of those that a mesh axis runs over, the one named last changes fastest.
Arguments:
- tokens: bfloat16 [1024, 7168], P('expert', 'dp'), may hold values from -6 to 6
- cotangent: bfloat16 [1024, 7168], P('expert', 'dp'), may hold values from -6 to 6
- expert_ids: int32 [1024, 8], P('expert'), may hold values from 0 to 15, all different within a row; in each aligned block of 64 rows (0 to 63, 64 to 127, ...) at most 40 rows name the same one
- gate_values: float32 [1024, 8], P('expert'), may hold values from 0.05 to 1
- gate_up_weight: bfloat16 [16, 2, 7168, 1024], P('expert', None, None, 'dp'), may hold values from -0.0625 to 0.0625
- down_weight: bfloat16 [16, 1024, 7168], P('expert', 'dp'), may hold values from -0.1875 to 0.1875
Outputs:
- output: bfloat16 [1024, 7168], P('expert', 'dp')
- input_grad: bfloat16 [1024, 7168], P('expert', 'dp')
- grad_gate_up: bfloat16 [16, 2, 7168, 1024], P('expert', None, None, 'dp')
- grad_down: bfloat16 [16, 1024, 7168], P('expert', 'dp')
The draws below stay inside these ranges and needn't reach their ends.
Inputs may be any that keep to these rules, and one draw needn't show every extreme that they name: `expert_ids`: each row names 8 different experts. Within the rows of one device (aligned blocks of 64 rows) no expert is named by more than 40 rows, and in some block one expert is named by exactly 40 rows.
All inputs are finite; a program needn't handle non-finite values.
Results may differ from the reference program's by a relative error of at most 0.013.
Values may be sent and summed in bfloat16 or wider, within the bound.
A program may use at most 192 MiB of HBM per device.

```python
import math
import jax
import jax.numpy as jnp
import numpy as np
from jax import lax

D = 7168
H = 1024
TOP = 8
TOKB = 64
EXPERTS = 16
CAP = 40
TOKENS = 1024
N_DP = 2


def shard_levels(rng, extent, pieces, least, top_value):
    gain = 1.0
    for dim, parts in pieces:
        draws = jax.random.uniform(jax.random.fold_in(jax.random.fold_in(rng, 6), dim), (parts,), jnp.float32, least / len(pieces), top_value / len(pieces))
        gain = gain * jnp.repeat(jnp.exp(draws), extent[dim] // parts).reshape((-1,) + (1,) * (len(extent) - 1 - dim))
    return gain


def shared_out(rng, own, number, rows, count, top, limit, skew):
    ranking = jax.random.permutation(rng, count)
    crowded, common = portions_of(count, rows * top, limit, skew, True), portions_of(count, rows * top, limit, skew, False)
    places = jnp.arange(count)

    def named(tallies, offset_by):
        used = int((tallies > 0).sum())
        fixed = max(1, used // 4)
        shifted = fixed + (places - fixed + offset_by * (used - fixed)) % max(1, count - fixed)
        return jnp.zeros((count,), jnp.int32).at[ranking[jnp.where(places < fixed, places, shifted)]].set(jnp.asarray(tallies, jnp.int32))

    tallies = jnp.where(number % 4 == 0, named(crowded, number // 4), named(common, number - number // 4 - 1))
    mixed = jax.random.permutation(jax.random.fold_in(own, 3), count)
    donor, taker = mixed[0:count // 2 * 2:2], mixed[1:count // 2 * 2:2]
    margin = jnp.minimum(tallies[donor] - 1, limit - tallies[taker]) // 2
    margin = jnp.where((donor == ranking[0]) | (taker == ranking[0]) | (tallies[taker] == 0), 0, jnp.maximum(margin, 0))
    shifted = jax.random.randint(jax.random.fold_in(own, 4), (count // 2,), 0, 1 << 20) % (margin + 1)
    tallies = tallies.at[donor].add(-shifted).at[taker].add(shifted)
    members = jnp.searchsorted(jnp.cumsum(tallies), jnp.arange(rows * top), side="right").astype(jnp.int32)
    grid = members.reshape(top, rows).T
    grid = grid[jax.random.permutation(jax.random.fold_in(own, 1), rows)]
    offset_by = jax.random.randint(jax.random.fold_in(own, 2), (rows, 1), 0, top)
    return jnp.take_along_axis(grid, (jnp.arange(top)[None, :] + offset_by) % top, axis=1)


def portions_of(amount, total, most, skew, full):
    loads = [(1 << 20) // math.isqrt(grade ** skew) + 1 for grade in range(1, amount + 1)]
    largest = most if full else min(most, max(-(-total // amount), total * loads[0] // sum(loads)))
    least = 1 if total - largest >= amount - 1 else 0
    given, spare = [largest] + [least] * (amount - 1), total - largest - least * (amount - 1)
    while spare > 0:
        movable = [i for i in range(1, amount) if given[i] < largest] or [i for i in range(1, amount) if given[i] < most]
        pool, remaining = sum([loads[i] for i in movable]), spare
        for i in movable:
            more = min(most - given[i], max(1, remaining * loads[i] // pool), spare)
            given[i] = given[i] + more
            spare = spare - more
    return np.array(given)


def bell_draw(rng, shape, scale, limit, pieces=(), kind=jnp.bfloat16):
    factor_of = shard_levels(rng, shape, pieces, -0.22, 0.18) if pieces else 1.0
    array = jax.random.normal(rng, shape, jnp.float32) * scale * factor_of
    return jnp.minimum(jnp.maximum(array, -limit), limit).astype(kind)


def setup_inputs(seed: int = 0) -> dict:
    seeds = jax.random.split(jax.random.key(seed), 7)
    tokens = bell_draw(seeds[0], (TOKENS, D), 1.0, 6.0, ((0, 16), (1, 2)))
    cotangent = bell_draw(seeds[1], (TOKENS, D), 1.0, 6.0, ((0, 16), (1, 2)))
    expert_ids_keys = jax.random.split(jax.random.fold_in(seeds[2], 1), TOKENS // TOKB)
    expert_ids_turns = jax.random.permutation(jax.random.fold_in(seeds[2], 3), TOKENS // TOKB)
    expert_ids = jax.vmap(lambda own, number: shared_out(jax.random.fold_in(seeds[2], 2), own, number, TOKB, EXPERTS, TOP, CAP, 2))(expert_ids_keys, expert_ids_turns).reshape((TOKENS, TOP))
    gate_values = jnp.clip(jnp.exp(math.log(1.0) - 2.9957323 * jax.random.uniform(seeds[3], (TOKENS, TOP), jnp.float32) ** shard_levels(seeds[3], (TOKENS, TOP), ((0, 16),), -0.2, 0.2)), 0.05, 1.0)
    gate_up_weight = bell_draw(seeds[4], (EXPERTS, 2, D, H), D ** -0.5, 0.0625, ((0, 16), (3, 2)))
    down_weight = bell_draw(seeds[5], (EXPERTS, H, D), H ** -0.5, 0.1875, ((0, 16), (1, 2)))
    return dict(tokens=tokens, cotangent=cotangent, expert_ids=expert_ids, gate_values=gate_values, gate_up_weight=gate_up_weight, down_weight=down_weight)


def reference(tokens, cotangent, expert_ids, gate_values, gate_up_weight, down_weight):
    token_count = TOKENS
    row_limit = EXPERTS * CAP
    group_width = H // N_DP

    def one_expert(running, inputs):
        out_acc, in_acc = running
        expert, gate_up_one, down_one = inputs
        chosen = expert_ids == expert
        weight = jnp.sum(jnp.where(chosen, gate_values, 0.0), axis=1)
        routed_here = jnp.any(chosen, axis=1)
        indices = jnp.arange(token_count, dtype=jnp.int32)
        sort_keys = jnp.where(routed_here, indices, indices + token_count)
        picked = jnp.argsort(sort_keys, stable=True)[:row_limit].astype(jnp.int32)
        live_rows = routed_here[picked]
        row_gate = jnp.where(live_rows, weight[picked], 0.0)
        rows_in = tokens[picked]
        gate_up_f = gate_up_one.astype(jnp.float32)
        down_f = down_one.astype(jnp.float32)
        pre = jnp.einsum("rd,cdh->rch", rows_in.astype(jnp.float32), gate_up_f)
        gate_pre = pre[:, 0]
        up_pre = pre[:, 1]
        sigmoid_gate = jax.nn.sigmoid(gate_pre)
        silu_gate = gate_pre * sigmoid_gate
        hidden = (silu_gate * up_pre).astype(jnp.bfloat16)
        hidden_groups = hidden.astype(jnp.float32).reshape(row_limit, N_DP, group_width)
        down_groups = down_f.reshape(N_DP, group_width, D)
        group_parts = jnp.einsum("rgh,ghd->grd", hidden_groups, down_groups).astype(jnp.bfloat16)
        out_rows = jnp.sum(group_parts.astype(jnp.float32), axis=0).astype(jnp.bfloat16)
        out_acc = out_acc.at[picked].add(row_gate[:, None] * out_rows.astype(jnp.float32))
        back = (row_gate[:, None] * cotangent[picked].astype(jnp.float32)).astype(jnp.bfloat16)
        back_f = back.astype(jnp.float32)
        grad_hidden = jnp.einsum("rd,hd->rh", back_f, down_f)
        grad_gate = (grad_hidden * up_pre * sigmoid_gate * (1.0 + gate_pre * (1.0 - sigmoid_gate))).astype(jnp.bfloat16)
        grad_up = (grad_hidden * silu_gate).astype(jnp.bfloat16)
        grad_pre = jnp.stack([grad_gate, grad_up], axis=1).astype(jnp.float32)
        grad_down_one = jnp.einsum("rh,rd->hd", hidden.astype(jnp.float32), back_f).astype(jnp.bfloat16)
        grad_gate_up_one = jnp.einsum("rd,rch->cdh", rows_in.astype(jnp.float32), grad_pre).astype(jnp.bfloat16)
        pre_groups = grad_pre.reshape(row_limit, 2, N_DP, group_width)
        weight_groups = gate_up_f.reshape(2, D, N_DP, group_width)
        in_parts = jnp.einsum("rcgh,cdgh->grd", pre_groups, weight_groups).astype(jnp.bfloat16)
        in_rows = jnp.sum(in_parts.astype(jnp.float32), axis=0).astype(jnp.bfloat16)
        in_acc = in_acc.at[picked].add(jnp.where(live_rows[:, None], in_rows.astype(jnp.float32), 0.0))
        return (out_acc, in_acc), (grad_gate_up_one, grad_down_one)

    start = (jnp.zeros((token_count, D), jnp.float32), jnp.zeros((token_count, D), jnp.float32))
    experts_list = jnp.arange(EXPERTS, dtype=jnp.int32)
    finals, grads = lax.scan(one_expert, start, (experts_list, gate_up_weight, down_weight))
    output = finals[0].astype(jnp.bfloat16)
    input_grad = finals[1].astype(jnp.bfloat16)
    return output, input_grad, grads[0], grads[1]
```

```python
import jax
import jax.numpy as jnp
from jax import lax
from jax.sharding import PartitionSpec as P


def expert_gates(expert_ids, gate_values, expert_count):
    named = expert_ids[:, :, None] == jnp.arange(expert_count, dtype=jnp.int32)
    return jnp.sum(jnp.where(named, gate_values[:, :, None], 0.0), axis=1)


def body(tokens, cotangent, expert_ids, gate_values, gate_up_weight, down_weight):
    expert_count = lax.axis_size("expert")
    parts = lax.axis_size("dp")
    rows, width = tokens.shape
    both = ("dp", "expert")
    f32 = jnp.float32
    bf16 = jnp.bfloat16
    gates = lax.all_gather(
        expert_gates(expert_ids, gate_values, expert_count), "expert", axis=0, tiled=True
    )
    gate = lax.dynamic_slice_in_dim(gates, lax.axis_index("expert"), 1, axis=1)
    gate_weight = gate_up_weight[0, 0]
    up_weight = gate_up_weight[0, 1]
    down = down_weight[0]
    spans = [slice(p * width, (p + 1) * width) for p in range(parts)]
    cols = (((1,), (1,)), ((), ()))
    over = (((0,), (0,)), ((), ()))

    def dot(x, y, dims=(((1,), (0,)), ((), ()))):
        return lax.dot_general(x, y, dims, preferred_element_type=f32)

    def gathered(x):
        return lax.all_gather(x, both, axis=0, tiled=False).reshape(parts, -1, width)

    def scattered(pieces):
        x = jnp.concatenate(pieces, axis=0).reshape(parts * expert_count, rows, width)
        return lax.psum_scatter(x, both, scatter_dimension=0, tiled=False)

    x = gathered(tokens)
    c = gathered(cotangent)
    a = sum(dot(x[p], gate_weight[spans[p]]) for p in range(parts))
    b = sum(dot(x[p], up_weight[spans[p]]) for p in range(parts))
    s = jax.nn.sigmoid(a)
    silu = a * s
    hidden = (silu * b).astype(bf16)
    output = scattered([(dot(hidden, down[:, span]) * gate).astype(bf16) for span in spans])
    back = [(c[p].astype(f32) * gate).astype(bf16) for p in range(parts)]
    grad_hidden = sum(dot(back[p], down[:, spans[p]], cols) for p in range(parts))
    grad_gate = (grad_hidden * b * s * (1.0 + a * (1.0 - s))).astype(bf16)
    grad_up = (grad_hidden * silu).astype(bf16)
    input_grad = scattered(
        [
            (
                dot(grad_gate, gate_weight[span], cols) + dot(grad_up, up_weight[span], cols)
            ).astype(bf16)
            for span in spans
        ]
    )
    grad_down = jnp.concatenate([dot(hidden, k, over).astype(bf16) for k in back], axis=1)
    grad_gate_up = jnp.stack(
        [
            jnp.concatenate([dot(x[p], g, over).astype(bf16) for p in range(parts)], axis=0)
            for g in (grad_gate, grad_up)
        ]
    )
    return (output, input_grad, grad_gate_up[None], grad_down[None])


def solution(mesh):
    return jax.shard_map(
        body,
        mesh=mesh,
        in_specs=(
            P("expert", "dp"),
            P("expert", "dp"),
            P("expert", None),
            P("expert", None),
            P("expert", None, None, "dp"),
            P("expert", "dp", None),
        ),
        out_specs=(
            P("expert", "dp"),
            P("expert", "dp"),
            P("expert", None, None, "dp"),
            P("expert", "dp", None),
        ),
        check_vma=False,
    )
```
